32 devices in a mesh: ctx: 8 (over z, y), fsdp: 4 (over x, core).
Axes of the slice: x: 2, y: 2, z: 4, core: 2. Of those that a mesh axis runs over, the one named last changes fastest.
Arguments:
- tokens: bfloat16 [4, 2048, 8192], P('fsdp', 'ctx'), may hold values from -6 to 6
- w_query: bfloat16 [8192, 512], P('fsdp'), may hold values from -0.125 to 0.125
- keys: bfloat16 [4, 2048, 128], P('fsdp', 'ctx'), may hold values from -512 to 512
- values: bfloat16 [4, 2048, 128], P('fsdp', 'ctx'), may hold values from -6 to 6
- gates: bfloat16 [4, 2048, 3], P('fsdp', 'ctx'), may hold values from 0.25 to 1
- routes: int32 [4, 2048, 2], P('fsdp', 'ctx'), may hold values from 0 to 2, all different within a row
- w_out: bfloat16 [512, 8192], P(None, 'fsdp'), may hold values from -1 to 1
Outputs:
- mixed: bfloat16 [4, 2048, 8192], P('fsdp', 'ctx')
The draws below stay inside these ranges and needn't reach their ends.
Inputs may be any that keep to these rules, and one draw needn't show every extreme that they name: `routes`: the 2 routed heads of a token differ.
All inputs are finite; a program needn't handle non-finite values.
Results may differ from the reference program's by a relative error of at most 0.035.
Values may be sent and summed in bfloat16 or wider, within the bound.
A program may use at most 128 MiB of HBM per device.

```python
import jax
import jax.numpy as jnp
from jax import lax

D = 8192
HS = 128
HG = 4
TOPK = 2
SEQS = 4
LEN = 2048


def draw_keys(key, part):
    full_shape = (SEQS, LEN, HS)
    return jax.random.normal(jax.random.fold_in(key, 1), full_shape, jnp.float32).astype(jnp.bfloat16)


def level_of(key, dims, cuts, smallest, high):
    level = 1.0
    for dim, shards_of in cuts:
        steps = jax.random.uniform(jax.random.fold_in(jax.random.fold_in(key, 6), dim), (shards_of,), jnp.float32, smallest / len(cuts), high / len(cuts))
        level = level * jnp.repeat(jnp.exp(steps), dims[dim] // shards_of).reshape((-1,) + (1,) * (len(dims) - 1 - dim))
    return level


def choose_distinct(key, rows, count, top, lift):
    sequence = jax.random.permutation(jax.random.fold_in(key, 1), count)
    pull = sequence
    for power in range(3):
        pull = pull * pull // count
    pull = pull * lift // count
    tickets = jax.random.randint(jax.random.fold_in(key, 2), (rows, count), 0, 4096) + pull
    sure = jax.random.permutation(jax.random.fold_in(key, 3), rows)[jnp.arange(count) % rows]
    tickets = jnp.where(jnp.arange(rows)[:, None] == sure[None, :], 1 << 14, tickets)
    score = tickets * count + jnp.arange(count)
    return lax.top_k(score.astype(jnp.int32), top)[1].astype(jnp.int32)


def gaussian(rng, shape, width, limit, shards=(), kind=jnp.bfloat16):
    entries = jax.random.normal(rng, shape, jnp.float32) * width
    if len(shards) > 0:
        entries = level_of(rng, shape, shards, -0.22, 0.18) * entries
    return jnp.clip(entries, min=-limit, max=limit).astype(kind)


def setup_inputs(seed: int = 0) -> dict:
    key_list = jax.random.split(jax.random.key(seed), 8)
    return {
        "tokens": gaussian(key_list[0], (SEQS, LEN, D), 1.0, 6.0, ((0, 4), (1, 8))),
        "w_query": gaussian(key_list[1], (D, HG * HS), (D // 4) ** -0.5, 0.125, ((0, 4),)),
        "keys": draw_keys(jax.random.fold_in(key_list[7], 71), 0),
        "values": gaussian(key_list[3], (SEQS, LEN, HS), 1.0, 6.0, ((0, 4), (1, 8))),
        "gates": jnp.clip(0.25 + 0.75 * jax.random.uniform(key_list[4], (SEQS, LEN, TOPK + 1), jnp.float32) ** level_of(key_list[4], (SEQS, LEN, TOPK + 1), ((0, 4), (1, 8)), -0.2, 0.2), 0.25, 1.0).astype(jnp.bfloat16),
        "routes": choose_distinct(key_list[5], SEQS * LEN, HG - 1, TOPK, 5461).reshape((SEQS, LEN, TOPK)),
        "w_out": gaussian(key_list[6], (HG * HS, D), (HG * HS // 16) ** -0.5, 1.0, ((1, 4),)),
    }


theta_base = 500000.0


def rotate(projected, positions, head_size):
    tok_rows = projected.shape[0]
    by_head = projected.reshape(tok_rows, -1, head_size)
    middle = head_size // 2
    inv_freq = jnp.power(theta_base, -2.0 * jnp.arange(middle, dtype=jnp.float32) / head_size)
    angles = positions[:, None] * inv_freq[None, :]
    cosine = jnp.cos(angles)[:, None, :]
    sine_part = jnp.sin(angles)[:, None, :]
    front_part = by_head[:, :, :middle]
    back_part = by_head[:, :, middle:]
    turned = jnp.concatenate([front_part * cosine - back_part * sine_part, back_part * cosine + front_part * sine_part], axis=2)
    return turned.reshape(tok_rows, -1)


def head_weights(gates, routes, head_count):
    gains = gates.astype(jnp.float32)
    head_index = jnp.arange(head_count, dtype=jnp.int32)[None, :]
    shared = (head_index == 0).astype(jnp.float32) * gains[:, 0:1]
    first_pick = (head_index == routes[:, 0:1] + 1).astype(jnp.float32) * gains[:, 1:2]
    second_pick = (head_index == routes[:, 1:2] + 1).astype(jnp.float32) * gains[:, 2:3]
    return shared + first_pick + second_pick


def reference(tokens, w_query, keys, values, gates, routes, w_out):
    head_size = keys.shape[2]
    head_count = w_query.shape[1] // head_size
    score_scale = head_size ** -0.5
    seq_len = tokens.shape[1]
    positions = jnp.arange(seq_len, dtype=jnp.float32)
    causal = jnp.arange(seq_len, dtype=jnp.int32)[None, :] <= jnp.arange(seq_len, dtype=jnp.int32)[:, None]

    def one_sequence(element):
        x_seq, key_seq, value_seq, gate_seq, route_seq = element
        projected = jnp.dot(x_seq, w_query, preferred_element_type=jnp.float32)
        queries = rotate(projected, positions, head_size).astype(jnp.bfloat16)
        mixing = head_weights(gate_seq, route_seq, head_count)

        def one_head(head_num):
            head_q = lax.dynamic_slice_in_dim(queries, head_num * head_size, head_size, 1)
            scores = jnp.dot(head_q, key_seq.T, preferred_element_type=jnp.float32) * score_scale
            row_max = jnp.max(jnp.where(causal, scores, -jnp.inf), axis=1)
            exp_terms = jnp.where(causal, jnp.exp(scores - row_max[:, None]), 0.0)
            denominator = jnp.sum(exp_terms, axis=1)
            soft_weights = exp_terms.astype(jnp.bfloat16)
            return jnp.dot(soft_weights, value_seq, preferred_element_type=jnp.float32) / denominator[:, None]

        attended = lax.map(one_head, jnp.arange(head_count, dtype=jnp.int32))
        hidden = (attended.transpose(1, 0, 2) * mixing[:, :, None]).reshape(seq_len, head_count * head_size).astype(jnp.bfloat16)
        return jnp.dot(hidden, w_out, preferred_element_type=jnp.float32).astype(jnp.bfloat16)

    return lax.map(one_sequence, (tokens, keys, values, gates, routes))
```

```python
import functools

import jax
import jax.numpy as jnp
import numpy as np
from jax import lax
from jax.experimental import pallas as pl
from jax.experimental.pallas import tpu as pltpu
from jax.sharding import PartitionSpec as P

theta_base = 500000.0
piece = 256
MESH = pl.DeviceIdType.MESH
QUERY, OUT = 0, 1
BY_X, BY_Y, CORE_X, CORE_Y = range(4)


def rotary_tables(rows, blocks, head_size):
    middle = head_size // 2
    freq = theta_base ** (-2.0 * np.arange(middle, dtype=np.float64) / head_size)
    freq = np.concatenate([freq, freq])[None, :]
    sign = np.where(np.arange(head_size) < middle, -1.0, 1.0)[None, :]

    def tables(positions):
        angles = positions[:, None].astype(np.float64) * freq
        return np.cos(angles).astype(np.float32), (sign * np.sin(angles)).astype(np.float32)

    return tables(np.arange(rows)) + tables(np.arange(blocks) * rows)


def kernel(
    ctx_size, fsdp_size, pieces,
    tok_hbm, wq_hbm, key_hbm, val_hbm, wo_hbm, gates_ref, routes_ref, cos_row, sin_row, cos_blk, sin_blk,
    out_hbm,
    tok, wq, wo, kv, acc, queries, hidden, out_buf,
    send_sem, recv_sem, own_send, own_recv, kv_send, kv_recv, load_sem, wo_load, out_sem,
):
    c = lax.axis_index("ctx")
    f = lax.axis_index("fsdp")
    core = lax.rem(f, 2)
    h = f // 2
    y = lax.rem(c, 2)
    z = c // 2
    chips = fsdp_size // 2
    pairs = ctx_size // 2
    rows = tok.shape[0]
    head_size = kv.shape[2] // 2
    head_count = queries.shape[1] // head_size
    c_mate = z * 2 + (1 - y)
    f_mate = h * 2 + (1 - core)

    def chip_at(d):
        return lax.rem(h + d + chips, chips) * 2 + core

    load_wq = [
        pltpu.make_async_copy(wq_hbm.at[half, s], wq.at[f, half, s], load_sem.at[4 + half * pieces + s])
        for half in range(2)
        for s in range(pieces)
    ]
    load_k = pltpu.make_async_copy(key_hbm, kv.at[c, :, pl.ds(0, head_size)], load_sem.at[0])
    load_v = pltpu.make_async_copy(val_hbm, kv.at[c, :, pl.ds(head_size, head_size)], load_sem.at[1])
    load_tok = pltpu.make_async_copy(tok_hbm, tok, load_sem.at[2])
    load_wo = [
        pltpu.make_async_copy(
            wo_hbm.at[:, pl.ds((half * pieces + s) * piece, piece)],
            wo.at[f, half, s],
            wo_load.at[half * pieces + s],
        )
        for half in range(2)
        for s in range(pieces)
    ]
    load_k.start()
    load_v.start()
    load_tok.start()
    for copy in load_wq + load_wo:
        copy.start()

    barrier = pltpu.get_barrier_semaphore()
    partners = [(c, f_mate), (c_mate, f)]
    partners += [(c, chip_at(d)) for d in range(1, chips)]
    partners += [(lax.rem(z + d, pairs) * 2 + y, f) for d in range(1, pairs)]
    for partner in partners:
        pl.semaphore_signal(barrier, inc=1, device_id=partner, device_id_type=MESH)
    pl.semaphore_wait(barrier, len(partners))

    def remote(src, dst, sem_s, sem_r, device):
        return pltpu.make_async_remote_copy(
            src_ref=src, dst_ref=dst, send_sem=sem_s, recv_sem=sem_r, device_id=device, device_id_type=MESH
        )

    def held(w, g, half, s):
        return (wq if w == QUERY else wo).at[g, half, s]

    def transfer(w, kind, d, s):
        g = chip_at(-d)
        sems = (send_sem.at[w, kind, d - 1, s], recv_sem.at[w, kind, d - 1, s])
        if kind == BY_X:
            here = wq_hbm.at[y, s] if w == QUERY else held(w, f, y, s)
            return remote(here, held(w, f, y, s), *sems, (c, chip_at(d)))
        half = y if kind == CORE_X or kind == BY_Y else 1 - y
        block = held(w, g, half, s)
        return remote(block, block, *sems, (c_mate, f) if kind == BY_Y else (c, f_mate))

    own_wq = [
        remote(wq_hbm.at[half], wq.at[f, half], own_send.at[QUERY, half], own_recv.at[QUERY, half], (c, f_mate))
        for half in range(2)
    ]
    own_wo = [
        remote(wo.at[f, half], wo.at[f, half], own_send.at[OUT, half], own_recv.at[OUT, half], (c, f_mate))
        for half in range(2)
    ]

    started = []

    def start(copy):
        copy.start()
        started.append(copy)

    stream = [(w, s) for w in (QUERY, OUT) for s in range(pieces)]

    def send_x(position):
        if position < len(stream):
            for d in range(1, chips):
                start(transfer(stream[position][0], BY_X, d, stream[position][1]))

    send_x(0)
    load_k.wait()
    load_v.wait()
    kv_mate = remote(kv.at[c], kv.at[c], kv_send.at[0, 0], kv_recv.at[c], (c_mate, f))
    kv_mate.start()
    for copy in own_wq:
        copy.start()
    for copy in load_wo:
        copy.wait()
    send_x(1)

    def kv_copy(which, block, zz):
        return remote(kv.at[block], kv.at[block], kv_send.at[which, zz], kv_recv.at[block], (zz * 2 + y, f))

    def kv_wait(block):
        remote(kv.at[block], kv.at[block], kv_send.at[0, 0], kv_recv.at[block], (c_mate, f)).wait_recv()

    def kv_spread(which, block):
        for zz in range(1, pairs):
            @pl.when(zz > z)
            def _():
                kv_copy(which, block, zz).start()

    kv_spread(0, c)

    def project(g, half, s, count):
        width = count * piece
        at = pl.multiple_of(((g * 2 + half) * pieces + s) * piece, piece)
        weight = wq[g, half, pl.ds(s, count)].reshape(width, acc.shape[1])
        return jnp.dot(tok[:, pl.ds(at, width)], weight, preferred_element_type=jnp.float32)

    load_tok.wait()
    for copy in load_wq:
        copy.wait()
    acc[...] = project(f, 0, 0, pieces)
    acc[...] += project(f, 1, 0, pieces)
    kv_wait(c_mate)
    kv_spread(1, c_mate)
    for half in range(2):
        own_wq[half].wait_recv()
        acc[...] += project(f_mate, half, 0, pieces)

    def arrive_x(w, s):
        for d in range(1, chips):
            transfer(w, BY_X, d, s).wait_recv()
            start(transfer(w, BY_Y, d, s))
            start(transfer(w, CORE_X, d, s))
        send_x(w * pieces + s + 2)

    def arrive_y(w, s):
        for d in range(1, chips):
            g = chip_at(-d)
            block = held(w, g, 1 - y, s)
            remote(
                block, block, send_sem.at[w, BY_Y, d - 1, s], recv_sem.at[w, BY_Y, d - 1, s], (c_mate, f)
            ).wait_recv()
            start(transfer(w, CORE_Y, d, s))

    def wait_piece(w, kind, d, s):
        g = lax.rem(h - d + chips, chips) * 2 + (1 - core)
        half = y if kind == CORE_X else 1 - y
        block = held(w, g, half, s)
        remote(
            block, block, send_sem.at[w, kind, d - 1, s], recv_sem.at[w, kind, d - 1, s], (c, f_mate)
        ).wait_recv()
        return g, half

    for t in range(pieces + 1):
        if t < pieces:
            arrive_x(QUERY, t)
        if t == pieces:
            arrive_x(OUT, 0)
        if t >= 1:
            arrive_y(QUERY, t - 1)
        if t < pieces:
            for d in range(1, chips):
                acc[...] += project(chip_at(-d), y, t, 1)
        if t >= 1:
            for d in range(1, chips):
                acc[...] += project(chip_at(-d), 1 - y, t - 1, 1)
            for d in range(1, chips):
                g, half = wait_piece(QUERY, CORE_X, d, t - 1)
                acc[...] += project(g, half, t - 1, 1)
        if t >= 2:
            for d in range(1, chips):
                g, half = wait_piece(QUERY, CORE_Y, d, t - 2)
                acc[...] += project(g, half, t - 2, 1)
    for d in range(1, chips):
        g, half = wait_piece(QUERY, CORE_Y, d, pieces - 1)
        acc[...] += project(g, half, pieces - 1, 1)
    for copy in own_wo:
        copy.start()

    cos_c, sin_c = cos_blk[pl.ds(c, 1), :], sin_blk[pl.ds(c, 1), :]
    cosine = cos_row[...] * cos_c - sin_row[...] * sin_c
    signed_sine = sin_row[...] * cos_c + cos_row[...] * sin_c
    for n in range(head_count):
        part = acc[:, n * head_size : (n + 1) * head_size]
        turned = part * cosine + pltpu.roll(part, head_size // 2, 1) * signed_sine
        queries[:, n * head_size : (n + 1) * head_size] = turned.astype(jnp.bfloat16)

    @pl.loop(0, z * 2)
    def _(block):
        kv_wait(block)

    to_log2 = float(head_size ** -0.5 * np.log2(np.e))
    gains = gates_ref[...].astype(jnp.float32)
    picks = routes_ref[...]

    def attend(n):
        q = queries[:, n * head_size : (n + 1) * head_size]

        def score(block):
            return (
                lax.dot_general(
                    q, kv[block, :, :head_size], (((1,), (1,)), ((), ())), preferred_element_type=jnp.float32
                )
                * to_log2
            )

        def weigh(block, terms):
            return jnp.dot(
                terms.astype(jnp.bfloat16), kv[block, :, head_size:], preferred_element_type=jnp.float32
            )

        own = score(c)
        row = lax.broadcasted_iota(jnp.int32, own.shape, 0)
        col = lax.broadcasted_iota(jnp.int32, own.shape, 1)
        own = jnp.where(col <= row, own, -1e30)
        top = jnp.max(own, axis=1, keepdims=True)
        terms = jnp.exp2(own - top)

        def step(block, carried):
            top, total, mix = carried
            here = score(block)
            new_top = jnp.maximum(top, jnp.max(here, axis=1, keepdims=True))
            factor = jnp.exp2(top - new_top)
            terms = jnp.exp2(here - new_top)
            total = total * factor + jnp.sum(terms, axis=1, keepdims=True)
            return new_top, total, mix * factor + weigh(block, terms)

        top, total, mix = lax.fori_loop(
            0, c, step, (top, jnp.sum(terms, axis=1, keepdims=True), weigh(c, terms))
        )
        if n == 0:
            gain = gains[:, 0:1]
        else:
            gain = jnp.where(picks[:, 0:1] + 1 == n, gains[:, 1:2], 0.0) + jnp.where(
                picks[:, 1:2] + 1 == n, gains[:, 2:3], 0.0
            )
        hidden[:, n * head_size : (n + 1) * head_size] = (mix / total * gain).astype(jnp.bfloat16)

    def serve(t):
        if t < pieces:
            arrive_x(OUT, t)
        if 1 <= t <= pieces:
            arrive_y(OUT, t - 1)

    served = 1
    for n in range(head_count):
        attend(n)
        if n % 2 == 1 and served <= pieces:
            serve(served)
            served += 1

    def emit(g, half, s):
        result = jnp.dot(hidden[...], wo[g, half, s], preferred_element_type=jnp.float32)
        at = pl.multiple_of(((g * 2 + half) * pieces + s) * piece, piece)
        out_buf[g, half, s] = result.astype(jnp.bfloat16)
        pltpu.make_async_copy(
            out_buf.at[g, half, s], out_hbm.at[:, pl.ds(at, piece)], out_sem.at[g, half, s]
        ).start()

    for half in range(2):
        for s in range(pieces):
            emit(f, half, s)
    for half in range(2):
        own_wo[half].wait_recv()
        for s in range(pieces):
            emit(f_mate, half, s)

    for t in range(pieces + 2):
        if t >= served:
            serve(t)
        for d in range(1, chips):
            if t < pieces:
                emit(chip_at(-d), y, t)
            if 1 <= t <= pieces:
                emit(chip_at(-d), 1 - y, t - 1)
                g, half = wait_piece(OUT, CORE_X, d, t - 1)
                emit(g, half, t - 1)
            if t >= 2:
                g, half = wait_piece(OUT, CORE_Y, d, t - 2)
                emit(g, half, t - 2)

    for copy in started + own_wq + own_wo + [kv_mate]:
        copy.wait_send()
    for which, block in ((0, c), (1, c_mate)):
        for zz in range(1, pairs):
            @pl.when(zz > z)
            def _():
                kv_copy(which, block, zz).wait_send()
    for g in range(fsdp_size):
        for half in range(2):
            for s in range(pieces):
                at = ((g * 2 + half) * pieces + s) * piece
                pltpu.make_async_copy(
                    out_buf.at[g, half, s], out_hbm.at[:, pl.ds(at, piece)], out_sem.at[g, half, s]
                ).wait()


def per_device(ctx_size, fsdp_size, tokens, w_query, keys, values, gates, routes, w_out):
    rows, width = tokens.shape[1:]
    depth, inner = w_query.shape
    head_size = keys.shape[2]
    pieces = depth // (2 * piece)
    chips = fsdp_size // 2
    pairs = ctx_size // 2
    tables = [jnp.asarray(t) for t in rotary_tables(rows, ctx_size, head_size)]
    anywhere = pl.BlockSpec(memory_space=pl.ANY)
    in_vmem = pl.BlockSpec(memory_space=pltpu.VMEM)
    bf16 = jnp.bfloat16
    dma = pltpu.SemaphoreType.DMA
    mixed = pl.pallas_call(
        functools.partial(kernel, ctx_size, fsdp_size, pieces),
        out_shape=jax.ShapeDtypeStruct((rows, width), bf16),
        in_specs=[anywhere] * 5 + [in_vmem] * 6,
        out_specs=anywhere,
        scratch_shapes=[
            pltpu.VMEM((rows, width), bf16),
            pltpu.VMEM((fsdp_size, 2, pieces, piece, inner), bf16),
            pltpu.VMEM((fsdp_size, 2, pieces, inner, piece), bf16),
            pltpu.VMEM((ctx_size, rows, 2 * head_size), bf16),
            pltpu.VMEM((rows, inner), jnp.float32),
            pltpu.VMEM((rows, inner), bf16),
            pltpu.VMEM((rows, inner), bf16),
            pltpu.VMEM((fsdp_size, 2, pieces, rows, piece), bf16),
            dma((2, 4, chips - 1, pieces)),
            dma((2, 4, chips - 1, pieces)),
            dma((2, 2)),
            dma((2, 2)),
            dma((2, pairs)),
            dma((ctx_size,)),
            dma((4 + 2 * pieces,)),
            dma((2 * pieces,)),
            dma((fsdp_size, 2, pieces)),
        ],
        compiler_params=pltpu.CompilerParams(
            collective_id=0, has_side_effects=True, vmem_limit_bytes=50 * 1024 * 1024
        ),
    )(
        tokens[0],
        w_query.reshape(2, pieces, piece, inner),
        keys[0],
        values[0],
        w_out,
        gates[0],
        routes[0],
        *tables,
    )
    return mixed[None]


def solution(mesh):
    in_specs = (
        P("fsdp", "ctx", None),
        P("fsdp", None),
        P("fsdp", "ctx", None),
        P("fsdp", "ctx", None),
        P("fsdp", "ctx", None),
        P("fsdp", "ctx", None),
        P(None, "fsdp"),
    )
    return jax.shard_map(
        functools.partial(per_device, mesh.shape["ctx"], mesh.shape["fsdp"]),
        mesh=mesh,
        in_specs=in_specs,
        out_specs=P("fsdp", "ctx", None),
        check_vma=False,
    )
```

```python
import functools

import jax
import jax.numpy as jnp
import numpy as np
from jax import lax
from jax.experimental import pallas as pl
from jax.experimental.pallas import tpu as pltpu
from jax.sharding import PartitionSpec as P

theta_base = 500000.0
piece = 256
MESH = pl.DeviceIdType.MESH
QUERY, OUT = 0, 1
BY_X, BY_Y, CORE_X, CORE_Y, BY_ZX, BY_ZY, CORE_ZX, CORE_ZY = range(8)


def rotary_tables(rows, blocks, head_size):
    middle = head_size // 2
    freq = theta_base ** (-2.0 * np.arange(middle, dtype=np.float64) / head_size)
    freq = np.concatenate([freq, freq])[None, :]
    sign = np.where(np.arange(head_size) < middle, -1.0, 1.0)[None, :]

    def tables(positions):
        angles = positions[:, None].astype(np.float64) * freq
        sine = np.sin(angles)
        return np.stack([np.cos(angles), sign * sine, sine]).astype(np.float32)

    return tables(np.arange(rows)), tables(np.arange(blocks) * rows)


def kernel(
    ctx_size, fsdp_size, pieces,
    tok_hbm, wq_hbm, key_hbm, val_hbm, wo_hbm, gates_ref, routes_hbm, row_hbm, blk_hbm,
    out_hbm,
    routes_ref, row_tab, blk_tab, tok, wq, wo, kv, acc, queries, hidden, out_buf,
    send_sem, recv_sem, own_send, own_recv, kv_send, kv_recv, load_sem, wo_load, out_sem, small_sem,
):
    c = lax.axis_index("ctx")
    f = lax.axis_index("fsdp")
    core = lax.rem(f, 2)
    h = f // 2
    y = lax.rem(c, 2)
    z = c // 2
    chips = fsdp_size // 2
    pairs = ctx_size // 2
    rows = tok.shape[0]
    head_size = kv.shape[2] // 2
    head_count = queries.shape[1] // head_size
    c_mate = z * 2 + (1 - y)
    f_mate = h * 2 + (1 - core)
    cube = pieces == 4 and pairs % 2 == 0
    z_bit = lax.rem(z, 2)
    c_next = (z + 1 - 2 * z_bit) * 2 + y
    roots = [2 + z_bit, 0, 1] if cube else list(range(pieces))
    steps = len(roots)
    z_root = 3 - z_bit

    def chip_at(d):
        return lax.rem(h + d + chips, chips) * 2 + core

    load_wq = [
        pltpu.make_async_copy(wq_hbm.at[half, s], wq.at[f, half, s], load_sem.at[4 + half * pieces + s])
        for half in range(2)
        for s in range(pieces)
    ]
    load_k = pltpu.make_async_copy(key_hbm, kv.at[c, :, pl.ds(0, head_size)], load_sem.at[0])
    load_v = pltpu.make_async_copy(val_hbm, kv.at[c, :, pl.ds(head_size, head_size)], load_sem.at[1])
    load_tok = pltpu.make_async_copy(tok_hbm, tok, load_sem.at[2])
    load_wo = [
        pltpu.make_async_copy(
            wo_hbm.at[:, pl.ds((half * pieces + s) * piece, piece)],
            wo.at[f, half, s],
            wo_load.at[half * pieces + s],
        )
        for half in range(2)
        for s in range(pieces)
    ]
    small = [
        pltpu.make_async_copy(source, target, small_sem.at[i])
        for i, (source, target) in enumerate(
            ((routes_hbm, routes_ref), (row_hbm, row_tab), (blk_hbm, blk_tab))
        )
    ]
    load_k.start()
    load_v.start()
    load_tok.start()
    for copy in load_wq + load_wo + small:
        copy.start()

    barrier = pltpu.get_barrier_semaphore()
    partners = [(c, f_mate), (c_mate, f)]
    partners += [(c, chip_at(d)) for d in range(1, chips)]
    partners += [(lax.rem(z + d, pairs) * 2 + y, f) for d in range(1, pairs)]
    for partner in partners:
        pl.semaphore_signal(barrier, inc=1, device_id=partner, device_id_type=MESH)
    pl.semaphore_wait(barrier, len(partners))

    def remote(src, dst, sem_s, sem_r, device):
        return pltpu.make_async_remote_copy(
            src_ref=src, dst_ref=dst, send_sem=sem_s, recv_sem=sem_r, device_id=device, device_id_type=MESH
        )

    def held(w, g, half, s):
        return (wq if w == QUERY else wo).at[g, half, s]

    def transfer(w, kind, d, t):
        s = z_root if kind in (CORE_ZX, CORE_ZY) else roots[t]
        sems = (send_sem.at[w, kind, d - 1, t], recv_sem.at[w, kind, d - 1, t])
        if kind == BY_X:
            here = wq_hbm.at[y, s] if w == QUERY else held(w, f, y, s)
            return remote(here, held(w, f, y, s), *sems, (c, chip_at(d)))
        half = y if kind in (BY_Y, CORE_X, BY_ZX, CORE_ZX) else 1 - y
        block = held(w, chip_at(-d), half, s)
        if kind == BY_Y:
            target = (c_mate, f)
        elif kind in (BY_ZX, BY_ZY):
            target = (c_next, f)
        else:
            target = (c, f_mate)
        return remote(block, block, *sems, target)

    def arrival(w, kind, d, t):
        s = z_root if kind in (BY_ZX, BY_ZY, CORE_ZX, CORE_ZY) else roots[t]
        from_core = kind in (CORE_X, CORE_Y, CORE_ZX, CORE_ZY)
        g = lax.rem(h - d + chips, chips) * 2 + ((1 - core) if from_core else core)
        half = y if kind in (BY_X, CORE_X, BY_ZX, CORE_ZX) else 1 - y
        block = held(w, g, half, s)
        remote(
            block, block, send_sem.at[w, kind, d - 1, t], recv_sem.at[w, kind, d - 1, t], (c, f_mate)
        ).wait_recv()
        return g, half, s

    own_wq = [
        remote(wq_hbm.at[half], wq.at[f, half], own_send.at[QUERY, half], own_recv.at[QUERY, half], (c, f_mate))
        for half in range(2)
    ]
    own_wo = [
        remote(wo.at[f, half], wo.at[f, half], own_send.at[OUT, half], own_recv.at[OUT, half], (c, f_mate))
        for half in range(2)
    ]

    started = []

    def start(copy):
        copy.start()
        started.append(copy)

    stream = [(w, s) for w in (QUERY, OUT) for s in range(steps)]

    def send_x(position):
        if position < len(stream):
            for d in range(1, chips):
                start(transfer(stream[position][0], BY_X, d, stream[position][1]))

    send_x(0)
    load_k.wait()
    load_v.wait()
    kv_mate = remote(kv.at[c], kv.at[c], kv_send.at[0, 0], kv_recv.at[c], (c_mate, f))
    kv_mate.start()
    for copy in own_wq:
        copy.start()
    for copy in load_wo:
        copy.wait()
    send_x(1)

    def kv_copy(which, block, zz):
        return remote(kv.at[block], kv.at[block], kv_send.at[which, zz], kv_recv.at[block], (zz * 2 + y, f))

    def kv_wait(block):
        remote(kv.at[block], kv.at[block], kv_send.at[0, 0], kv_recv.at[block], (c_mate, f)).wait_recv()

    def kv_spread(which, block):
        for zz in range(1, pairs):
            @pl.when(zz > z)
            def _():
                kv_copy(which, block, zz).start()

    kv_spread(0, c)

    def project(g, half, s, count):
        width = count * piece
        at = pl.multiple_of(((g * 2 + half) * pieces + s) * piece, piece)
        weight = wq[g, half, pl.ds(s, count)].reshape(width, acc.shape[1])
        return jnp.dot(tok[:, pl.ds(at, width)], weight, preferred_element_type=jnp.float32)

    load_tok.wait()
    for copy in load_wq:
        copy.wait()
    acc[...] = project(f, 0, 0, pieces)
    acc[...] += project(f, 1, 0, pieces)
    for half in range(2):
        own_wq[half].wait_recv()
        acc[...] += project(f_mate, half, 0, pieces)

    def come(w, kind, t, forwards):
        landed = []
        for d in range(1, chips):
            landed.append(arrival(w, kind, d, t))
            for onward in forwards:
                start(transfer(w, onward, d, t))
        return landed

    def serve(w, t):
        landed = []
        if t < steps:
            landed += come(w, BY_X, t, ([BY_ZX] if cube and t == 0 else []) + [BY_Y, CORE_X])
            send_x(w * steps + t + 2)
        if 1 <= t <= steps:
            landed += come(w, BY_Y, t - 1, ([BY_ZY] if cube and t == 1 else []) + [CORE_Y])
        if cube and t == 2:
            landed += come(w, BY_ZX, 0, [CORE_ZX])
        if cube and t == 3:
            landed += come(w, BY_ZY, 0, [CORE_ZY])
        return landed

    def gather_core(w, t):
        landed = []
        t -= 1
        if 0 <= t < steps:
            landed += come(w, CORE_X, t, [])
        if 1 <= t <= steps:
            landed += come(w, CORE_Y, t - 1, [])
        if cube and t == 2:
            landed += come(w, CORE_ZX, 0, [])
        if cube and t == 3:
            landed += come(w, CORE_ZY, 0, [])
        return landed

    for t in range(steps + 2):
        landed = serve(QUERY, t)
        if t == steps:
            out_landed = serve(OUT, 0)
        if t == min(1, steps):
            kv_wait(c_mate)
            kv_spread(1, c_mate)
        for g, half, s in landed:
            acc[...] += project(g, half, s, 1)
        for g, half, s in gather_core(QUERY, t):
            acc[...] += project(g, half, s, 1)
    for copy in own_wo:
        copy.start()

    for copy in small:
        copy.wait()
    cos_c, sin_c = blk_tab[0, pl.ds(c, 1), :], blk_tab[1, pl.ds(c, 1), :]
    plain_c = blk_tab[2, pl.ds(c, 1), :]
    cosine = row_tab[0] * cos_c - row_tab[2] * plain_c
    signed_sine = row_tab[1] * cos_c + row_tab[0] * sin_c
    for n in range(head_count):
        part = acc[:, n * head_size : (n + 1) * head_size]
        turned = part * cosine + pltpu.roll(part, head_size // 2, 1) * signed_sine
        queries[:, n * head_size : (n + 1) * head_size] = turned.astype(jnp.bfloat16)

    @pl.loop(0, z * 2)
    def _(block):
        kv_wait(block)

    to_log2 = float(head_size ** -0.5 * np.log2(np.e))
    gains = gates_ref[...].astype(jnp.float32)
    picks = routes_ref[...]
    by_head = [gains[0:1, :]] + [
        jnp.where(picks[0:1, :] + 1 == n, gains[1:2, :], 0.0)
        + jnp.where(picks[1:2, :] + 1 == n, gains[2:3, :], 0.0)
        for n in range(1, head_count)
    ]
    by_head += [jnp.zeros_like(by_head[0])] * (8 - head_count)
    mixing = jnp.concatenate(by_head, axis=0).T

    def attend(n):
        q = queries[:, n * head_size : (n + 1) * head_size]

        def score(block):
            return (
                lax.dot_general(
                    q, kv[block, :, :head_size], (((1,), (1,)), ((), ())), preferred_element_type=jnp.float32
                )
                * to_log2
            )

        def weigh(block, terms):
            return jnp.dot(
                terms.astype(jnp.bfloat16), kv[block, :, head_size:], preferred_element_type=jnp.float32
            )

        own = score(c)
        row = lax.broadcasted_iota(jnp.int32, own.shape, 0)
        col = lax.broadcasted_iota(jnp.int32, own.shape, 1)
        own = jnp.where(col <= row, own, -1e30)
        top = jnp.max(own, axis=1, keepdims=True)
        terms = jnp.exp2(own - top)

        def step(block, carried):
            top, total, mix = carried
            here = score(block)
            new_top = jnp.maximum(top, jnp.max(here, axis=1, keepdims=True))
            factor = jnp.exp2(top - new_top)
            terms = jnp.exp2(here - new_top)
            total = total * factor + jnp.sum(terms, axis=1, keepdims=True)
            return new_top, total, mix * factor + weigh(block, terms)

        top, total, mix = lax.fori_loop(
            0, c, step, (top, jnp.sum(terms, axis=1, keepdims=True), weigh(c, terms))
        )
        gain = mixing[:, n : n + 1]
        hidden[:, n * head_size : (n + 1) * head_size] = (mix / total * gain).astype(jnp.bfloat16)

    served = 1
    for n in range(head_count):
        attend(n)
        if n % 2 == 1 and served <= steps:
            out_landed += serve(OUT, served)
            served += 1

    def emit(g, half, s):
        result = jnp.dot(hidden[...], wo[g, half, s], preferred_element_type=jnp.float32)
        at = pl.multiple_of(((g * 2 + half) * pieces + s) * piece, piece)
        out_buf[g, half, s] = result.astype(jnp.bfloat16)
        pltpu.make_async_copy(
            out_buf.at[g, half, s], out_hbm.at[:, pl.ds(at, piece)], out_sem.at[g, half, s]
        ).start()

    for half in range(2):
        for s in range(pieces):
            emit(f, half, s)
    for half in range(2):
        own_wo[half].wait_recv()
        for s in range(pieces):
            emit(f_mate, half, s)

    for t in range(steps + 2):
        if t >= served:
            out_landed = serve(OUT, t)
        if t >= served - 1:
            for g, half, s in out_landed:
                emit(g, half, s)
        for g, half, s in gather_core(OUT, t):
            emit(g, half, s)

    for copy in started + own_wq + own_wo + [kv_mate]:
        copy.wait_send()
    for which, block in ((0, c), (1, c_mate)):
        for zz in range(1, pairs):
            @pl.when(zz > z)
            def _():
                kv_copy(which, block, zz).wait_send()
    for g in range(fsdp_size):
        for half in range(2):
            for s in range(pieces):
                at = ((g * 2 + half) * pieces + s) * piece
                pltpu.make_async_copy(
                    out_buf.at[g, half, s], out_hbm.at[:, pl.ds(at, piece)], out_sem.at[g, half, s]
                ).wait()


def per_device(ctx_size, fsdp_size, tokens, w_query, keys, values, gates, routes, w_out):
    rows, width = tokens.shape[1:]
    depth, inner = w_query.shape
    head_size = keys.shape[2]
    pieces = depth // (2 * piece)
    chips = fsdp_size // 2
    pairs = ctx_size // 2
    tables = [jnp.asarray(t) for t in rotary_tables(rows, ctx_size, head_size)]
    anywhere = pl.BlockSpec(memory_space=pl.ANY)
    bf16 = jnp.bfloat16
    dma = pltpu.SemaphoreType.DMA
    mixed = pl.pallas_call(
        functools.partial(kernel, ctx_size, fsdp_size, pieces),
        out_shape=jax.ShapeDtypeStruct((rows, width), bf16),
        in_specs=[anywhere] * 5 + [pl.BlockSpec(memory_space=pltpu.VMEM)] + [anywhere] * 3,
        out_specs=anywhere,
        scratch_shapes=[
            pltpu.VMEM((routes.shape[2], rows), jnp.int32),
            pltpu.VMEM(tables[0].shape, jnp.float32),
            pltpu.VMEM(tables[1].shape, jnp.float32),
            pltpu.VMEM((rows, width), bf16),
            pltpu.VMEM((fsdp_size, 2, pieces, piece, inner), bf16),
            pltpu.VMEM((fsdp_size, 2, pieces, inner, piece), bf16),
            pltpu.VMEM((ctx_size, rows, 2 * head_size), bf16),
            pltpu.VMEM((rows, inner), jnp.float32),
            pltpu.VMEM((rows, inner), bf16),
            pltpu.VMEM((rows, inner), bf16),
            pltpu.VMEM((fsdp_size, 2, pieces, rows, piece), bf16),
            dma((2, 8, chips - 1, pieces)),
            dma((2, 8, chips - 1, pieces)),
            dma((2, 2)),
            dma((2, 2)),
            dma((2, pairs)),
            dma((ctx_size,)),
            dma((4 + 2 * pieces,)),
            dma((2 * pieces,)),
            dma((fsdp_size, 2, pieces)),
            dma((3,)),
        ],
        compiler_params=pltpu.CompilerParams(
            collective_id=0, has_side_effects=True, vmem_limit_bytes=62 * 1024 * 1024
        ),
    )(
        tokens[0],
        w_query.reshape(2, pieces, piece, inner),
        keys[0],
        values[0],
        w_out,
        gates[0].T,
        routes[0].T,
        *tables,
    )
    return mixed[None]


def solution(mesh):
    in_specs = (
        P("fsdp", "ctx", None),
        P("fsdp", None),
        P("fsdp", "ctx", None),
        P("fsdp", "ctx", None),
        P("fsdp", "ctx", None),
        P("fsdp", "ctx", None),
        P(None, "fsdp"),
    )
    return jax.shard_map(
        functools.partial(per_device, mesh.shape["ctx"], mesh.shape["fsdp"]),
        mesh=mesh,
        in_specs=in_specs,
        out_specs=P("fsdp", "ctx", None),
        check_vma=False,
    )
```

```python
import functools

import jax
import jax.numpy as jnp
import numpy as np
from jax import lax
from jax.experimental import pallas as pl
from jax.experimental.pallas import tpu as pltpu
from jax.sharding import PartitionSpec as P

theta_base = 500000.0
piece = 256
MESH = pl.DeviceIdType.MESH
QUERY, OUT = 0, 1
BY_X, BY_Y, CORE_X, CORE_Y, BY_ZX, BY_ZY, CORE_ZX, CORE_ZY = range(8)


def rotary_tables(rows, blocks, head_size):
    middle = head_size // 2
    freq = theta_base ** (-2.0 * np.arange(middle, dtype=np.float64) / head_size)
    freq = np.concatenate([freq, freq])[None, :]
    sign = np.where(np.arange(head_size) < middle, -1.0, 1.0)[None, :]

    def tables(positions):
        angles = positions[:, None].astype(np.float64) * freq
        sine = np.sin(angles)
        return np.stack([np.cos(angles), sign * sine, sine]).astype(np.float32)

    return tables(np.arange(rows)), tables(np.arange(blocks) * rows)


def kernel(
    ctx_size, fsdp_size, pieces,
    tok_hbm, wq_hbm, key_hbm, val_hbm, wo_hbm, gates_ref, routes_hbm, row_hbm, blk_hbm,
    out_hbm,
    routes_ref, row_tab, blk_tab, tok, wq, wo, kv, acc, queries, hidden, out_buf,
    send_sem, recv_sem, own_send, own_recv, kv_send, kv_recv, load_sem, wo_load, out_sem, small_sem,
):
    c = lax.axis_index("ctx")
    f = lax.axis_index("fsdp")
    core = lax.rem(f, 2)
    h = f // 2
    y = lax.rem(c, 2)
    z = c // 2
    chips = fsdp_size // 2
    pairs = ctx_size // 2
    rows = tok.shape[0]
    head_size = kv.shape[2] // 2
    head_count = queries.shape[1] // head_size
    c_mate = z * 2 + (1 - y)
    f_mate = h * 2 + (1 - core)
    cube = pieces == 4 and pairs % 2 == 0
    z_bit = lax.rem(z, 2)
    c_next = (z + 1 - 2 * z_bit) * 2 + y
    roots = [2 + z_bit, 0, 1] if cube else list(range(pieces))
    steps = len(roots)
    z_root = 3 - z_bit

    def chip_at(d):
        return lax.rem(h + d + chips, chips) * 2 + core

    load_wq = [
        pltpu.make_async_copy(wq_hbm.at[half, s], wq.at[f, half, s], load_sem.at[4 + half * pieces + s])
        for half in range(2)
        for s in range(pieces)
    ]
    load_k = pltpu.make_async_copy(key_hbm, kv.at[c, :, pl.ds(0, head_size)], load_sem.at[0])
    load_v = pltpu.make_async_copy(val_hbm, kv.at[c, :, pl.ds(head_size, head_size)], load_sem.at[1])
    load_tok = pltpu.make_async_copy(tok_hbm, tok, load_sem.at[2])
    load_wo = [
        pltpu.make_async_copy(
            wo_hbm.at[:, pl.ds((half * pieces + s) * piece, piece)],
            wo.at[f, half, s],
            wo_load.at[half * pieces + s],
        )
        for half in range(2)
        for s in range(pieces)
    ]
    small = [
        pltpu.make_async_copy(source, target, small_sem.at[i])
        for i, (source, target) in enumerate(
            ((routes_hbm, routes_ref), (row_hbm, row_tab), (blk_hbm, blk_tab))
        )
    ]
    load_k.start()
    load_v.start()
    load_tok.start()
    for copy in load_wq + load_wo + small:
        copy.start()

    barrier = pltpu.get_barrier_semaphore()
    partners = [(c, f_mate), (c_mate, f)]
    partners += [(c, chip_at(d)) for d in range(1, chips)]
    partners += [(lax.rem(z + d, pairs) * 2 + y, f) for d in range(1, pairs)]
    for partner in partners:
        pl.semaphore_signal(barrier, inc=1, device_id=partner, device_id_type=MESH)
    pl.semaphore_wait(barrier, len(partners))

    def remote(src, dst, sem_s, sem_r, device):
        return pltpu.make_async_remote_copy(
            src_ref=src, dst_ref=dst, send_sem=sem_s, recv_sem=sem_r, device_id=device, device_id_type=MESH
        )

    def held(w, g, half, s):
        return (wq if w == QUERY else wo).at[g, half, s]

    def transfer(w, kind, d, t):
        s = z_root if kind in (CORE_ZX, CORE_ZY) else roots[t]
        sems = (send_sem.at[w, kind, d - 1, t], recv_sem.at[w, kind, d - 1, t])
        if kind == BY_X:
            here = wq_hbm.at[y, s] if w == QUERY else held(w, f, y, s)
            return remote(here, held(w, f, y, s), *sems, (c, chip_at(d)))
        half = y if kind in (BY_Y, CORE_X, BY_ZX, CORE_ZX) else 1 - y
        block = held(w, chip_at(-d), half, s)
        if kind == BY_Y:
            target = (c_mate, f)
        elif kind in (BY_ZX, BY_ZY):
            target = (c_next, f)
        else:
            target = (c, f_mate)
        return remote(block, block, *sems, target)

    def arrival(w, kind, d, t):
        s = z_root if kind in (BY_ZX, BY_ZY, CORE_ZX, CORE_ZY) else roots[t]
        from_core = kind in (CORE_X, CORE_Y, CORE_ZX, CORE_ZY)
        g = lax.rem(h - d + chips, chips) * 2 + ((1 - core) if from_core else core)
        half = y if kind in (BY_X, CORE_X, BY_ZX, CORE_ZX) else 1 - y
        block = held(w, g, half, s)
        remote(
            block, block, send_sem.at[w, kind, d - 1, t], recv_sem.at[w, kind, d - 1, t], (c, f_mate)
        ).wait_recv()
        return g, half, s

    own_wq = [
        remote(wq_hbm.at[half], wq.at[f, half], own_send.at[QUERY, half], own_recv.at[QUERY, half], (c, f_mate))
        for half in range(2)
    ]
    own_wo = [
        remote(wo.at[f, half], wo.at[f, half], own_send.at[OUT, half], own_recv.at[OUT, half], (c, f_mate))
        for half in range(2)
    ]

    started = []

    def start(copy):
        copy.start()
        started.append(copy)

    stream = [(w, s) for w in (QUERY, OUT) for s in range(steps)]

    def send_x(position):
        if position < len(stream):
            for d in range(1, chips):
                start(transfer(stream[position][0], BY_X, d, stream[position][1]))

    send_x(0)
    load_k.wait()
    load_v.wait()
    kv_mate = remote(kv.at[c], kv.at[c], kv_send.at[0, 0], kv_recv.at[c], (c_mate, f))
    kv_mate.start()
    for copy in own_wq:
        copy.start()
    for copy in load_wo:
        copy.wait()
    send_x(1)

    def kv_copy(which, block, zz):
        return remote(kv.at[block], kv.at[block], kv_send.at[which, zz], kv_recv.at[block], (zz * 2 + y, f))

    def kv_wait(block):
        remote(kv.at[block], kv.at[block], kv_send.at[0, 0], kv_recv.at[block], (c_mate, f)).wait_recv()

    def kv_spread(which, block):
        for zz in reversed(range(1, pairs)):
            @pl.when(zz > z)
            def _():
                kv_copy(which, block, zz).start()

    kv_spread(0, c)

    def project(g, half, s, count):
        width = count * piece
        at = pl.multiple_of(((g * 2 + half) * pieces + s) * piece, piece)
        weight = wq[g, half, pl.ds(s, count)].reshape(width, acc.shape[1])
        return jnp.dot(tok[:, pl.ds(at, width)], weight, preferred_element_type=jnp.float32)

    kv_wait(c_mate)
    kv_spread(1, c_mate)
    load_tok.wait()
    for copy in load_wq:
        copy.wait()
    acc[...] = project(f, 0, 0, pieces)
    acc[...] += project(f, 1, 0, pieces)
    for half in range(2):
        own_wq[half].wait_recv()
        acc[...] += project(f_mate, half, 0, pieces)

    def come(w, kind, t, forwards):
        landed = []
        for d in range(1, chips):
            landed.append(arrival(w, kind, d, t))
            for onward in forwards:
                start(transfer(w, onward, d, t))
        return landed

    def serve(w, t):
        landed = []
        if t < steps:
            landed += come(w, BY_X, t, ([BY_ZX] if cube and t == 0 else []) + [BY_Y, CORE_X])
            send_x(w * steps + t + 2)
        if 1 <= t <= steps:
            landed += come(w, BY_Y, t - 1, ([BY_ZY] if cube and t == 1 else []) + [CORE_Y])
        if cube and t == 2:
            landed += come(w, BY_ZX, 0, [CORE_ZX])
        if cube and t == 3:
            landed += come(w, BY_ZY, 0, [CORE_ZY])
        return landed

    def gather_core(w, t):
        landed = []
        t -= 1
        if 0 <= t < steps:
            landed += come(w, CORE_X, t, [])
        if 1 <= t <= steps:
            landed += come(w, CORE_Y, t - 1, [])
        if cube and t == 2:
            landed += come(w, CORE_ZX, 0, [])
        if cube and t == 3:
            landed += come(w, CORE_ZY, 0, [])
        return landed

    for t in range(steps + 2):
        landed = serve(QUERY, t)
        if t == steps:
            out_landed = serve(OUT, 0)
        for g, half, s in landed:
            acc[...] += project(g, half, s, 1)
        for g, half, s in gather_core(QUERY, t):
            acc[...] += project(g, half, s, 1)
    for copy in own_wo:
        copy.start()

    for copy in small:
        copy.wait()
    cos_c, sin_c = blk_tab[0, pl.ds(c, 1), :], blk_tab[1, pl.ds(c, 1), :]
    plain_c = blk_tab[2, pl.ds(c, 1), :]
    cosine = row_tab[0] * cos_c - row_tab[2] * plain_c
    signed_sine = row_tab[1] * cos_c + row_tab[0] * sin_c
    for n in range(head_count):
        part = acc[:, n * head_size : (n + 1) * head_size]
        turned = part * cosine + pltpu.roll(part, head_size // 2, 1) * signed_sine
        queries[:, n * head_size : (n + 1) * head_size] = turned.astype(jnp.bfloat16)

    @pl.loop(0, z * 2)
    def _(block):
        kv_wait(block)

    to_log2 = float(head_size ** -0.5 * np.log2(np.e))
    gains = gates_ref[...].astype(jnp.float32)
    picks = routes_ref[...]
    by_head = [gains[0:1, :]] + [
        jnp.where(picks[0:1, :] + 1 == n, gains[1:2, :], 0.0)
        + jnp.where(picks[1:2, :] + 1 == n, gains[2:3, :], 0.0)
        for n in range(1, head_count)
    ]
    by_head += [jnp.zeros_like(by_head[0])] * (8 - head_count)
    mixing = jnp.concatenate(by_head, axis=0).T

    def attend(n):
        q = queries[:, n * head_size : (n + 1) * head_size]

        def score(block):
            return (
                lax.dot_general(
                    q, kv[block, :, :head_size], (((1,), (1,)), ((), ())), preferred_element_type=jnp.float32
                )
                * to_log2
            )

        def weigh(block, terms):
            return jnp.dot(
                terms.astype(jnp.bfloat16), kv[block, :, head_size:], preferred_element_type=jnp.float32
            )

        own = score(c)
        row = lax.broadcasted_iota(jnp.int32, own.shape, 0)
        col = lax.broadcasted_iota(jnp.int32, own.shape, 1)
        own = jnp.where(col <= row, own, -1e30)
        top = jnp.max(own, axis=1, keepdims=True)
        terms = jnp.exp2(own - top)

        def step(block, carried):
            top, total, mix = carried
            here = score(block)
            new_top = jnp.maximum(top, jnp.max(here, axis=1, keepdims=True))
            factor = jnp.exp2(top - new_top)
            terms = jnp.exp2(here - new_top)
            total = total * factor + jnp.sum(terms, axis=1, keepdims=True)
            return new_top, total, mix * factor + weigh(block, terms)

        top, total, mix = lax.fori_loop(
            0, c, step, (top, jnp.sum(terms, axis=1, keepdims=True), weigh(c, terms))
        )
        gain = mixing[:, n : n + 1]
        hidden[:, n * head_size : (n + 1) * head_size] = (mix / total * gain).astype(jnp.bfloat16)

    served = 1
    for n in range(head_count):
        attend(n)
        if n % 2 == 1 and served <= steps:
            out_landed += serve(OUT, served)
            served += 1

    def emit(g, half, s):
        result = jnp.dot(hidden[...], wo[g, half, s], preferred_element_type=jnp.float32)
        at = pl.multiple_of(((g * 2 + half) * pieces + s) * piece, piece)
        out_buf[g, half, s] = result.astype(jnp.bfloat16)
        pltpu.make_async_copy(
            out_buf.at[g, half, s], out_hbm.at[:, pl.ds(at, piece)], out_sem.at[g, half, s]
        ).start()

    for half in range(2):
        for s in range(pieces):
            emit(f, half, s)
    for half in range(2):
        own_wo[half].wait_recv()
        for s in range(pieces):
            emit(f_mate, half, s)

    for t in range(steps + 2):
        if t >= served:
            out_landed = serve(OUT, t)
        if t >= served - 1:
            for g, half, s in out_landed:
                emit(g, half, s)
        for g, half, s in gather_core(OUT, t):
            emit(g, half, s)

    for copy in started + own_wq + own_wo + [kv_mate]:
        copy.wait_send()
    for which, block in ((0, c), (1, c_mate)):
        for zz in range(1, pairs):
            @pl.when(zz > z)
            def _():
                kv_copy(which, block, zz).wait_send()
    for g in range(fsdp_size):
        for half in range(2):
            for s in range(pieces):
                at = ((g * 2 + half) * pieces + s) * piece
                pltpu.make_async_copy(
                    out_buf.at[g, half, s], out_hbm.at[:, pl.ds(at, piece)], out_sem.at[g, half, s]
                ).wait()


def per_device(ctx_size, fsdp_size, tokens, w_query, keys, values, gates, routes, w_out):
    rows, width = tokens.shape[1:]
    depth, inner = w_query.shape
    head_size = keys.shape[2]
    pieces = depth // (2 * piece)
    chips = fsdp_size // 2
    pairs = ctx_size // 2
    tables = [jnp.asarray(t) for t in rotary_tables(rows, ctx_size, head_size)]
    anywhere = pl.BlockSpec(memory_space=pl.ANY)
    bf16 = jnp.bfloat16
    dma = pltpu.SemaphoreType.DMA
    mixed = pl.pallas_call(
        functools.partial(kernel, ctx_size, fsdp_size, pieces),
        out_shape=jax.ShapeDtypeStruct((rows, width), bf16),
        in_specs=[anywhere] * 5 + [pl.BlockSpec(memory_space=pltpu.VMEM)] + [anywhere] * 3,
        out_specs=anywhere,
        scratch_shapes=[
            pltpu.VMEM((routes.shape[2], rows), jnp.int32),
            pltpu.VMEM(tables[0].shape, jnp.float32),
            pltpu.VMEM(tables[1].shape, jnp.float32),
            pltpu.VMEM((rows, width), bf16),
            pltpu.VMEM((fsdp_size, 2, pieces, piece, inner), bf16),
            pltpu.VMEM((fsdp_size, 2, pieces, inner, piece), bf16),
            pltpu.VMEM((ctx_size, rows, 2 * head_size), bf16),
            pltpu.VMEM((rows, inner), jnp.float32),
            pltpu.VMEM((rows, inner), bf16),
            pltpu.VMEM((rows, inner), bf16),
            pltpu.VMEM((fsdp_size, 2, pieces, rows, piece), bf16),
            dma((2, 8, chips - 1, pieces)),
            dma((2, 8, chips - 1, pieces)),
            dma((2, 2)),
            dma((2, 2)),
            dma((2, pairs)),
            dma((ctx_size,)),
            dma((4 + 2 * pieces,)),
            dma((2 * pieces,)),
            dma((fsdp_size, 2, pieces)),
            dma((3,)),
        ],
        compiler_params=pltpu.CompilerParams(
            collective_id=0, has_side_effects=True, vmem_limit_bytes=62 * 1024 * 1024
        ),
    )(
        tokens[0],
        w_query.reshape(2, pieces, piece, inner),
        keys[0],
        values[0],
        w_out,
        gates[0].T,
        routes[0].T,
        *tables,
    )
    return mixed[None]


def solution(mesh):
    in_specs = (
        P("fsdp", "ctx", None),
        P("fsdp", None),
        P("fsdp", "ctx", None),
        P("fsdp", "ctx", None),
        P("fsdp", "ctx", None),
        P("fsdp", "ctx", None),
        P(None, "fsdp"),
    )
    return jax.shard_map(
        functools.partial(per_device, mesh.shape["ctx"], mesh.shape["fsdp"]),
        mesh=mesh,
        in_specs=in_specs,
        out_specs=P("fsdp", "ctx", None),
        check_vma=False,
    )
```

```python
import functools

import jax
import jax.numpy as jnp
import numpy as np
from jax import lax
from jax.experimental import pallas as pl
from jax.experimental.pallas import tpu as pltpu
from jax.sharding import PartitionSpec as P

theta_base = 500000.0
piece = 256
MESH = pl.DeviceIdType.MESH
QUERY, OUT = 0, 1
BY_X, BY_Y, CORE_X, CORE_Y, BY_ZX, BY_ZY, CORE_ZX, CORE_ZY = range(8)


def rotary_tables(rows, blocks, head_size):
    middle = head_size // 2
    freq = theta_base ** (-2.0 * np.arange(middle, dtype=np.float64) / head_size)
    freq = np.concatenate([freq, freq])[None, :]
    sign = np.where(np.arange(head_size) < middle, -1.0, 1.0)[None, :]

    def tables(positions):
        angles = positions[:, None].astype(np.float64) * freq
        sine = np.sin(angles)
        return np.stack([np.cos(angles), sign * sine, sine]).astype(np.float32)

    return tables(np.arange(rows)), tables(np.arange(blocks) * rows)


def kernel(
    ctx_size, fsdp_size, pieces,
    tok_hbm, wq_hbm, key_hbm, val_hbm, wo_hbm, gates_ref, routes_hbm, row_hbm, blk_hbm,
    out_hbm,
    routes_ref, row_tab, blk_tab, tok, wq, wo, kv, acc, queries, hidden, out_buf,
    send_sem, recv_sem, own_send, own_recv, kv_send, kv_recv, load_sem, wo_load, out_sem, small_sem,
):
    c = lax.axis_index("ctx")
    f = lax.axis_index("fsdp")
    core = lax.rem(f, 2)
    h = f // 2
    y = lax.rem(c, 2)
    z = c // 2
    chips = fsdp_size // 2
    pairs = ctx_size // 2
    rows = tok.shape[0]
    head_size = kv.shape[2] // 2
    head_count = queries.shape[1] // head_size
    c_mate = z * 2 + (1 - y)
    f_mate = h * 2 + (1 - core)
    cube = pieces == 4 and pairs % 2 == 0
    z_bit = lax.rem(z, 2)
    c_next = (z + 1 - 2 * z_bit) * 2 + y
    roots = [2 + z_bit, 0, 1] if cube else list(range(pieces))
    steps = len(roots)
    z_root = 3 - z_bit

    def chip_at(d):
        return lax.rem(h + d + chips, chips) * 2 + core

    load_wq = [
        pltpu.make_async_copy(wq_hbm.at[half, s], wq.at[f, half, s], load_sem.at[4 + half * pieces + s])
        for half in range(2)
        for s in range(pieces)
    ]
    load_k = pltpu.make_async_copy(key_hbm, kv.at[c, :, pl.ds(0, head_size)], load_sem.at[0])
    load_v = pltpu.make_async_copy(val_hbm, kv.at[c, :, pl.ds(head_size, head_size)], load_sem.at[1])
    load_tok = pltpu.make_async_copy(tok_hbm, tok, load_sem.at[2])
    load_wo = [
        pltpu.make_async_copy(
            wo_hbm.at[:, pl.ds((half * pieces + s) * piece, piece)],
            wo.at[f, half, s],
            wo_load.at[half * pieces + s],
        )
        for half in range(2)
        for s in range(pieces)
    ]
    small = [
        pltpu.make_async_copy(source, target, small_sem.at[i])
        for i, (source, target) in enumerate(
            ((routes_hbm, routes_ref), (row_hbm, row_tab), (blk_hbm, blk_tab))
        )
    ]
    load_k.start()
    load_v.start()
    load_tok.start()
    for copy in load_wq + load_wo + small:
        copy.start()

    barrier = pltpu.get_barrier_semaphore()
    partners = [(c, f_mate), (c_mate, f)]
    partners += [(c, chip_at(d)) for d in range(1, chips)]
    partners += [(lax.rem(z + d, pairs) * 2 + y, f) for d in range(1, pairs)]
    for partner in partners:
        pl.semaphore_signal(barrier, inc=1, device_id=partner, device_id_type=MESH)
    pl.semaphore_wait(barrier, len(partners))

    def remote(src, dst, sem_s, sem_r, device):
        return pltpu.make_async_remote_copy(
            src_ref=src, dst_ref=dst, send_sem=sem_s, recv_sem=sem_r, device_id=device, device_id_type=MESH
        )

    def held(w, g, half, s):
        return (wq if w == QUERY else wo).at[g, half, s]

    def transfer(w, kind, d, t):
        s = z_root if kind in (CORE_ZX, CORE_ZY) else roots[t]
        sems = (send_sem.at[w, kind, d - 1, t], recv_sem.at[w, kind, d - 1, t])
        if kind == BY_X:
            here = wq_hbm.at[y, s] if w == QUERY else held(w, f, y, s)
            return remote(here, held(w, f, y, s), *sems, (c, chip_at(d)))
        half = y if kind in (BY_Y, CORE_X, BY_ZX, CORE_ZX) else 1 - y
        block = held(w, chip_at(-d), half, s)
        if kind == BY_Y:
            target = (c_mate, f)
        elif kind in (BY_ZX, BY_ZY):
            target = (c_next, f)
        else:
            target = (c, f_mate)
        return remote(block, block, *sems, target)

    def arrival(w, kind, d, t):
        s = z_root if kind in (BY_ZX, BY_ZY, CORE_ZX, CORE_ZY) else roots[t]
        from_core = kind in (CORE_X, CORE_Y, CORE_ZX, CORE_ZY)
        g = lax.rem(h - d + chips, chips) * 2 + ((1 - core) if from_core else core)
        half = y if kind in (BY_X, CORE_X, BY_ZX, CORE_ZX) else 1 - y
        block = held(w, g, half, s)
        remote(
            block, block, send_sem.at[w, kind, d - 1, t], recv_sem.at[w, kind, d - 1, t], (c, f_mate)
        ).wait_recv()
        return g, half, s

    own_wq = [
        remote(wq_hbm.at[half], wq.at[f, half], own_send.at[QUERY, half], own_recv.at[QUERY, half], (c, f_mate))
        for half in range(2)
    ]
    own_wo = [
        remote(wo.at[f, half], wo.at[f, half], own_send.at[OUT, half], own_recv.at[OUT, half], (c, f_mate))
        for half in range(2)
    ]

    started = []

    def start(copy):
        copy.start()
        started.append(copy)

    stream = [(w, s) for w in (QUERY, OUT) for s in range(steps)]

    def send_x(position):
        if position < len(stream):
            for d in range(1, chips):
                start(transfer(stream[position][0], BY_X, d, stream[position][1]))

    send_x(0)
    load_k.wait()
    load_v.wait()
    kv_mate = remote(kv.at[c], kv.at[c], kv_send.at[0, 0], kv_recv.at[c], (c_mate, f))
    kv_mate.start()
    for copy in own_wq:
        copy.start()
    for copy in load_wo:
        copy.wait()
    send_x(1)

    def kv_copy(which, block, zz):
        return remote(kv.at[block], kv.at[block], kv_send.at[which, zz], kv_recv.at[block], (zz * 2 + y, f))

    def kv_wait(block):
        remote(kv.at[block], kv.at[block], kv_send.at[0, 0], kv_recv.at[block], (c_mate, f)).wait_recv()

    def kv_spread(which, block):
        for zz in range(1, pairs):
            @pl.when(zz > z)
            def _():
                kv_copy(which, block, zz).start()

    kv_spread(0, c)

    def project(g, half, s, count):
        width = count * piece
        at = pl.multiple_of(((g * 2 + half) * pieces + s) * piece, piece)
        weight = wq[g, half, pl.ds(s, count)].reshape(width, acc.shape[1])
        return jnp.dot(tok[:, pl.ds(at, width)], weight, preferred_element_type=jnp.float32)

    load_tok.wait()
    for copy in load_wq:
        copy.wait()
    acc[...] = project(f, 0, 0, pieces)
    acc[...] += project(f, 1, 0, pieces)
    for half in range(2):
        own_wq[half].wait_recv()
        acc[...] += project(f_mate, half, 0, pieces)

    def come(w, kind, t, forwards):
        landed = []
        for d in range(1, chips):
            landed.append(arrival(w, kind, d, t))
            for onward in forwards:
                start(transfer(w, onward, d, t))
        return landed

    def serve(w, t):
        landed = []
        if t < steps:
            landed += come(w, BY_X, t, ([BY_ZX] if cube and t == 0 else []) + [BY_Y, CORE_X])
            send_x(w * steps + t + 2)
        if 1 <= t <= steps:
            landed += come(w, BY_Y, t - 1, ([BY_ZY] if cube and t == 1 else []) + [CORE_Y])
        if cube and t == 2:
            landed += come(w, BY_ZX, 0, [CORE_ZX])
        if cube and t == 3:
            landed += come(w, BY_ZY, 0, [CORE_ZY])
        return landed

    def gather_core(w, t):
        landed = []
        t -= 1
        if 0 <= t < steps:
            landed += come(w, CORE_X, t, [])
        if 1 <= t <= steps:
            landed += come(w, CORE_Y, t - 1, [])
        if cube and t == 2:
            landed += come(w, CORE_ZX, 0, [])
        if cube and t == 3:
            landed += come(w, CORE_ZY, 0, [])
        return landed

    for t in range(steps + 2):
        landed = serve(QUERY, t)
        if t == steps:
            out_landed = serve(OUT, 0)
        if t == min(1, steps):
            kv_wait(c_mate)
            kv_spread(1, c_mate)
        for g, half, s in landed:
            acc[...] += project(g, half, s, 1)
        for g, half, s in gather_core(QUERY, t):
            acc[...] += project(g, half, s, 1)
    for copy in own_wo:
        copy.start()

    for copy in small:
        copy.wait()
    cos_c, sin_c = blk_tab[0, pl.ds(c, 1), :], blk_tab[1, pl.ds(c, 1), :]
    plain_c = blk_tab[2, pl.ds(c, 1), :]
    cosine = row_tab[0] * cos_c - row_tab[2] * plain_c
    signed_sine = row_tab[1] * cos_c + row_tab[0] * sin_c
    for n in range(head_count):
        part = acc[:, n * head_size : (n + 1) * head_size]
        turned = part * cosine + pltpu.roll(part, head_size // 2, 1) * signed_sine
        queries[:, n * head_size : (n + 1) * head_size] = turned.astype(jnp.bfloat16)

    out_landed += serve(OUT, 1)
    served = 2

    @pl.loop(0, z * 2)
    def _(block):
        kv_wait(block)

    to_log2 = float(head_size ** -0.5 * np.log2(np.e))
    gains = gates_ref[...].astype(jnp.float32)
    picks = routes_ref[...]
    by_head = [gains[0:1, :]] + [
        jnp.where(picks[0:1, :] + 1 == n, gains[1:2, :], 0.0)
        + jnp.where(picks[1:2, :] + 1 == n, gains[2:3, :], 0.0)
        for n in range(1, head_count)
    ]
    by_head += [jnp.zeros_like(by_head[0])] * (8 - head_count)
    mixing = jnp.concatenate(by_head, axis=0).T

    def attend(n):
        q = queries[:, n * head_size : (n + 1) * head_size]

        def score(block):
            return (
                lax.dot_general(
                    q, kv[block, :, :head_size], (((1,), (1,)), ((), ())), preferred_element_type=jnp.float32
                )
                * to_log2
            )

        def weigh(block, terms):
            return jnp.dot(
                terms.astype(jnp.bfloat16), kv[block, :, head_size:], preferred_element_type=jnp.float32
            )

        own = score(c)
        row = lax.broadcasted_iota(jnp.int32, own.shape, 0)
        col = lax.broadcasted_iota(jnp.int32, own.shape, 1)
        own = jnp.where(col <= row, own, -1e30)
        top = jnp.max(own, axis=1, keepdims=True)
        terms = jnp.exp2(own - top)

        def step(block, carried):
            top, total, mix = carried
            here = score(block)
            new_top = jnp.maximum(top, jnp.max(here, axis=1, keepdims=True))
            factor = jnp.exp2(top - new_top)
            terms = jnp.exp2(here - new_top)
            total = total * factor + jnp.sum(terms, axis=1, keepdims=True)
            return new_top, total, mix * factor + weigh(block, terms)

        top, total, mix = lax.fori_loop(
            0, c, step, (top, jnp.sum(terms, axis=1, keepdims=True), weigh(c, terms))
        )
        gain = mixing[:, n : n + 1]
        hidden[:, n * head_size : (n + 1) * head_size] = (mix / total * gain).astype(jnp.bfloat16)

    for n in range(head_count):
        attend(n)
        if n == 1 and served <= steps:
            out_landed += serve(OUT, served)
            served += 1

    def emit(g, half, s):
        result = jnp.dot(hidden[...], wo[g, half, s], preferred_element_type=jnp.float32)
        at = pl.multiple_of(((g * 2 + half) * pieces + s) * piece, piece)
        out_buf[g, half, s] = result.astype(jnp.bfloat16)
        pltpu.make_async_copy(
            out_buf.at[g, half, s], out_hbm.at[:, pl.ds(at, piece)], out_sem.at[g, half, s]
        ).start()

    for half in range(2):
        for s in range(pieces):
            emit(f, half, s)
    if served <= steps:
        out_landed += serve(OUT, served)
        served += 1
    for half in range(2):
        own_wo[half].wait_recv()
        for s in range(pieces):
            emit(f_mate, half, s)

    for g, half, s in out_landed:
        emit(g, half, s)
    for t in range(steps + 2):
        if t >= served:
            for g, half, s in serve(OUT, t):
                emit(g, half, s)
        for g, half, s in gather_core(OUT, t):
            emit(g, half, s)

    for copy in started + own_wq + own_wo + [kv_mate]:
        copy.wait_send()
    for which, block in ((0, c), (1, c_mate)):
        for zz in range(1, pairs):
            @pl.when(zz > z)
            def _():
                kv_copy(which, block, zz).wait_send()
    for g in range(fsdp_size):
        for half in range(2):
            for s in range(pieces):
                at = ((g * 2 + half) * pieces + s) * piece
                pltpu.make_async_copy(
                    out_buf.at[g, half, s], out_hbm.at[:, pl.ds(at, piece)], out_sem.at[g, half, s]
                ).wait()


def per_device(ctx_size, fsdp_size, tokens, w_query, keys, values, gates, routes, w_out):
    rows, width = tokens.shape[1:]
    depth, inner = w_query.shape
    head_size = keys.shape[2]
    pieces = depth // (2 * piece)
    chips = fsdp_size // 2
    pairs = ctx_size // 2
    tables = [jnp.asarray(t) for t in rotary_tables(rows, ctx_size, head_size)]
    anywhere = pl.BlockSpec(memory_space=pl.ANY)
    bf16 = jnp.bfloat16
    dma = pltpu.SemaphoreType.DMA
    mixed = pl.pallas_call(
        functools.partial(kernel, ctx_size, fsdp_size, pieces),
        out_shape=jax.ShapeDtypeStruct((rows, width), bf16),
        in_specs=[anywhere] * 5 + [pl.BlockSpec(memory_space=pltpu.VMEM)] + [anywhere] * 3,
        out_specs=anywhere,
        scratch_shapes=[
            pltpu.VMEM((routes.shape[2], rows), jnp.int32),
            pltpu.VMEM(tables[0].shape, jnp.float32),
            pltpu.VMEM(tables[1].shape, jnp.float32),
            pltpu.VMEM((rows, width), bf16),
            pltpu.VMEM((fsdp_size, 2, pieces, piece, inner), bf16),
            pltpu.VMEM((fsdp_size, 2, pieces, inner, piece), bf16),
            pltpu.VMEM((ctx_size, rows, 2 * head_size), bf16),
            pltpu.VMEM((rows, inner), jnp.float32),
            pltpu.VMEM((rows, inner), bf16),
            pltpu.VMEM((rows, inner), bf16),
            pltpu.VMEM((fsdp_size, 2, pieces, rows, piece), bf16),
            dma((2, 8, chips - 1, pieces)),
            dma((2, 8, chips - 1, pieces)),
            dma((2, 2)),
            dma((2, 2)),
            dma((2, pairs)),
            dma((ctx_size,)),
            dma((4 + 2 * pieces,)),
            dma((2 * pieces,)),
            dma((fsdp_size, 2, pieces)),
            dma((3,)),
        ],
        compiler_params=pltpu.CompilerParams(
            collective_id=0, has_side_effects=True, vmem_limit_bytes=62 * 1024 * 1024
        ),
    )(
        tokens[0],
        w_query.reshape(2, pieces, piece, inner),
        keys[0],
        values[0],
        w_out,
        gates[0].T,
        routes[0].T,
        *tables,
    )
    return mixed[None]


def solution(mesh):
    in_specs = (
        P("fsdp", "ctx", None),
        P("fsdp", None),
        P("fsdp", "ctx", None),
        P("fsdp", "ctx", None),
        P("fsdp", "ctx", None),
        P("fsdp", "ctx", None),
        P(None, "fsdp"),
    )
    return jax.shard_map(
        functools.partial(per_device, mesh.shape["ctx"], mesh.shape["fsdp"]),
        mesh=mesh,
        in_specs=in_specs,
        out_specs=P("fsdp", "ctx", None),
        check_vma=False,
    )
```

```python
import functools

import jax
import jax.numpy as jnp
import numpy as np
from jax import lax
from jax.experimental import pallas as pl
from jax.experimental.pallas import tpu as pltpu
from jax.sharding import PartitionSpec as P

theta_base = 500000.0
piece = 256
MESH = pl.DeviceIdType.MESH
QUERY, OUT = 0, 1
BY_X, BY_Y, CORE_X, CORE_Y, BY_ZX, BY_ZY, CORE_ZX, CORE_ZY = range(8)


def rotary_tables(rows, blocks, head_size):
    middle = head_size // 2
    freq = theta_base ** (-2.0 * np.arange(middle, dtype=np.float64) / head_size)
    freq = np.concatenate([freq, freq])[None, :]
    sign = np.where(np.arange(head_size) < middle, -1.0, 1.0)[None, :]

    def tables(positions):
        angles = positions[:, None].astype(np.float64) * freq
        sine = np.sin(angles)
        return np.stack([np.cos(angles), sign * sine, sine]).astype(np.float32)

    return tables(np.arange(rows)), tables(np.arange(blocks) * rows)


def kernel(
    ctx_size, fsdp_size, pieces,
    tok_hbm, wq_hbm, key_hbm, val_hbm, wo_hbm, gates_ref, routes_hbm, row_hbm, blk_hbm,
    out_hbm,
    routes_ref, row_tab, blk_tab, tok, wq, wo, kv, acc, queries, hidden, out_buf,
    send_sem, recv_sem, own_send, own_recv, kv_send, kv_recv, load_sem, wo_load, out_sem, small_sem,
):
    c = lax.axis_index("ctx")
    f = lax.axis_index("fsdp")
    core = lax.rem(f, 2)
    h = f // 2
    y = lax.rem(c, 2)
    z = c // 2
    chips = fsdp_size // 2
    pairs = ctx_size // 2
    rows = tok.shape[0]
    head_size = kv.shape[2] // 2
    head_count = queries.shape[1] // head_size
    c_mate = z * 2 + (1 - y)
    f_mate = h * 2 + (1 - core)
    cube = pieces == 4 and pairs % 2 == 0
    z_bit = lax.rem(z, 2)
    c_next = (z + 1 - 2 * z_bit) * 2 + y
    roots = [2 + z_bit, 0, 1] if cube else list(range(pieces))
    steps = len(roots)
    z_root = 3 - z_bit

    def chip_at(d):
        return lax.rem(h + d + chips, chips) * 2 + core

    load_wq = [
        pltpu.make_async_copy(wq_hbm.at[half, s], wq.at[f, half, s], load_sem.at[4 + half * pieces + s])
        for half in range(2)
        for s in range(pieces)
    ]
    load_k = pltpu.make_async_copy(key_hbm, kv.at[c, :, pl.ds(0, head_size)], load_sem.at[0])
    load_v = pltpu.make_async_copy(val_hbm, kv.at[c, :, pl.ds(head_size, head_size)], load_sem.at[1])
    load_tok = pltpu.make_async_copy(tok_hbm, tok, load_sem.at[2])
    load_wo = [
        pltpu.make_async_copy(
            wo_hbm.at[:, pl.ds((half * pieces + s) * piece, piece)],
            wo.at[f, half, s],
            wo_load.at[half * pieces + s],
        )
        for half in range(2)
        for s in range(pieces)
    ]
    small = [
        pltpu.make_async_copy(source, target, small_sem.at[i])
        for i, (source, target) in enumerate(
            ((routes_hbm, routes_ref), (row_hbm, row_tab), (blk_hbm, blk_tab))
        )
    ]
    load_k.start()
    load_v.start()
    load_tok.start()
    for copy in load_wq + load_wo + small:
        copy.start()

    barrier = pltpu.get_barrier_semaphore()
    partners = [(c, f_mate), (c_mate, f)]
    partners += [(c, chip_at(d)) for d in range(1, chips)]
    partners += [(lax.rem(z + d, pairs) * 2 + y, f) for d in range(1, pairs)]
    for partner in partners:
        pl.semaphore_signal(barrier, inc=1, device_id=partner, device_id_type=MESH)
    pl.semaphore_wait(barrier, len(partners))

    def remote(src, dst, sem_s, sem_r, device):
        return pltpu.make_async_remote_copy(
            src_ref=src, dst_ref=dst, send_sem=sem_s, recv_sem=sem_r, device_id=device, device_id_type=MESH
        )

    def held(w, g, half, s):
        return (wq if w == QUERY else wo).at[g, half, s]

    def transfer(w, kind, d, t):
        s = z_root if kind in (CORE_ZX, CORE_ZY) else roots[t]
        sems = (send_sem.at[w, kind, d - 1, t], recv_sem.at[w, kind, d - 1, t])
        if kind == BY_X:
            here = wq_hbm.at[y, s] if w == QUERY else held(w, f, y, s)
            return remote(here, held(w, f, y, s), *sems, (c, chip_at(d)))
        half = y if kind in (BY_Y, CORE_X, BY_ZX, CORE_ZX) else 1 - y
        block = held(w, chip_at(-d), half, s)
        if kind == BY_Y:
            target = (c_mate, f)
        elif kind in (BY_ZX, BY_ZY):
            target = (c_next, f)
        else:
            target = (c, f_mate)
        return remote(block, block, *sems, target)

    def arrival(w, kind, d, t):
        s = z_root if kind in (BY_ZX, BY_ZY, CORE_ZX, CORE_ZY) else roots[t]
        from_core = kind in (CORE_X, CORE_Y, CORE_ZX, CORE_ZY)
        g = lax.rem(h - d + chips, chips) * 2 + ((1 - core) if from_core else core)
        half = y if kind in (BY_X, CORE_X, BY_ZX, CORE_ZX) else 1 - y
        block = held(w, g, half, s)
        remote(
            block, block, send_sem.at[w, kind, d - 1, t], recv_sem.at[w, kind, d - 1, t], (c, f_mate)
        ).wait_recv()
        return g, half, s

    own_wq = [
        remote(wq_hbm.at[half], wq.at[f, half], own_send.at[QUERY, half], own_recv.at[QUERY, half], (c, f_mate))
        for half in range(2)
    ]
    own_wo = [
        remote(wo.at[f, half], wo.at[f, half], own_send.at[OUT, half], own_recv.at[OUT, half], (c, f_mate))
        for half in range(2)
    ]

    started = []

    def start(copy):
        copy.start()
        started.append(copy)

    stream = [(w, s) for w in (QUERY, OUT) for s in range(steps)]

    def send_x(position):
        if position < len(stream):
            for d in range(1, chips):
                start(transfer(stream[position][0], BY_X, d, stream[position][1]))

    send_x(0)
    load_k.wait()
    load_v.wait()
    kv_mate = remote(kv.at[c], kv.at[c], kv_send.at[0, 0], kv_recv.at[c], (c_mate, f))
    kv_mate.start()
    for copy in own_wq:
        copy.start()
    for copy in load_wo:
        copy.wait()
    send_x(1)

    def kv_copy(which, block, zz):
        return remote(kv.at[block], kv.at[block], kv_send.at[which, zz], kv_recv.at[block], (zz * 2 + y, f))

    def kv_wait(block):
        remote(kv.at[block], kv.at[block], kv_send.at[0, 0], kv_recv.at[block], (c_mate, f)).wait_recv()

    def kv_spread(which, block):
        for zz in range(1, pairs):
            @pl.when(zz > z)
            def _():
                kv_copy(which, block, zz).start()

    kv_spread(0, c)

    def project(g, half, s, count):
        width = count * piece
        at = pl.multiple_of(((g * 2 + half) * pieces + s) * piece, piece)
        weight = wq[g, half, pl.ds(s, count)].reshape(width, acc.shape[1])
        return jnp.dot(tok[:, pl.ds(at, width)], weight, preferred_element_type=jnp.float32)

    load_tok.wait()
    for copy in load_wq:
        copy.wait()
    acc[...] = project(f, 0, 0, pieces)
    acc[...] += project(f, 1, 0, pieces)
    for half in range(2):
        own_wq[half].wait_recv()
        acc[...] += project(f_mate, half, 0, pieces)

    def come(w, kind, t, forwards):
        landed = []
        for d in range(1, chips):
            landed.append(arrival(w, kind, d, t))
            for onward in forwards:
                start(transfer(w, onward, d, t))
        return landed

    def serve(w, t):
        landed = []
        if t < steps:
            landed += come(w, BY_X, t, ([BY_ZX] if cube and t == 0 else []) + [BY_Y, CORE_X])
            send_x(w * steps + t + 2)
        if 1 <= t <= steps:
            landed += come(w, BY_Y, t - 1, ([BY_ZY] if cube and t == 1 else []) + [CORE_Y])
        if cube and t == 2:
            landed += come(w, BY_ZX, 0, [CORE_ZX])
        if cube and t == 3:
            landed += come(w, BY_ZY, 0, [CORE_ZY])
        return landed

    def gather_core(w, t):
        landed = []
        t -= 1
        if 0 <= t < steps:
            landed += come(w, CORE_X, t, [])
        if 1 <= t <= steps:
            landed += come(w, CORE_Y, t - 1, [])
        if cube and t == 2:
            landed += come(w, CORE_ZX, 0, [])
        if cube and t == 3:
            landed += come(w, CORE_ZY, 0, [])
        return landed

    for t in range(steps + 2):
        landed = serve(QUERY, t)
        if t == steps:
            out_landed = serve(OUT, 0)
        if t == min(1, steps):
            kv_wait(c_mate)
            kv_spread(1, c_mate)
        for g, half, s in landed:
            acc[...] += project(g, half, s, 1)
        for g, half, s in gather_core(QUERY, t):
            acc[...] += project(g, half, s, 1)
    for copy in own_wo:
        copy.start()

    for copy in small:
        copy.wait()
    cos_c, sin_c = blk_tab[0, pl.ds(c, 1), :], blk_tab[1, pl.ds(c, 1), :]
    plain_c = blk_tab[2, pl.ds(c, 1), :]
    cosine = row_tab[0] * cos_c - row_tab[2] * plain_c
    signed_sine = row_tab[1] * cos_c + row_tab[0] * sin_c
    for n in range(head_count):
        part = acc[:, n * head_size : (n + 1) * head_size]
        turned = part * cosine + pltpu.roll(part, head_size // 2, 1) * signed_sine
        queries[:, n * head_size : (n + 1) * head_size] = turned.astype(jnp.bfloat16)

    out_landed += serve(OUT, 1)
    served = 2

    to_log2 = float(head_size ** -0.5 * np.log2(np.e))
    gains = gates_ref[...].astype(jnp.float32)
    picks = routes_ref[...]
    by_head = [gains[0:1, :]] + [
        jnp.where(picks[0:1, :] + 1 == n, gains[1:2, :], 0.0)
        + jnp.where(picks[1:2, :] + 1 == n, gains[2:3, :], 0.0)
        for n in range(1, head_count)
    ]
    by_head += [jnp.zeros_like(by_head[0])] * (8 - head_count)
    mixing = jnp.concatenate(by_head, axis=0).T

    def attend(n):
        q = queries[:, n * head_size : (n + 1) * head_size]

        def score(block):
            return (
                lax.dot_general(
                    q, kv[block, :, :head_size], (((1,), (1,)), ((), ())), preferred_element_type=jnp.float32
                )
                * to_log2
            )

        def weigh(block, terms):
            return jnp.dot(
                terms.astype(jnp.bfloat16), kv[block, :, head_size:], preferred_element_type=jnp.float32
            )

        own = score(c)
        row = lax.broadcasted_iota(jnp.int32, own.shape, 0)
        col = lax.broadcasted_iota(jnp.int32, own.shape, 1)
        own = jnp.where(col <= row, own, -1e30)
        top = jnp.max(own, axis=1, keepdims=True)
        terms = jnp.exp2(own - top)

        def step(i, carried):
            top, total, mix = carried
            block = c - 1 - i
            if n == 0:

                @pl.when(block < z * 2)
                def _():
                    kv_wait(block)

            here = score(block)
            new_top = jnp.maximum(top, jnp.max(here, axis=1, keepdims=True))
            factor = jnp.exp2(top - new_top)
            terms = jnp.exp2(here - new_top)
            total = total * factor + jnp.sum(terms, axis=1, keepdims=True)
            return new_top, total, mix * factor + weigh(block, terms)

        top, total, mix = lax.fori_loop(
            0, c, step, (top, jnp.sum(terms, axis=1, keepdims=True), weigh(c, terms))
        )
        gain = mixing[:, n : n + 1]
        hidden[:, n * head_size : (n + 1) * head_size] = (mix / total * gain).astype(jnp.bfloat16)

    for n in range(head_count):
        attend(n)
        if n == 1 and served <= steps:
            out_landed += serve(OUT, served)
            served += 1

    def emit(g, half, s):
        result = jnp.dot(hidden[...], wo[g, half, s], preferred_element_type=jnp.float32)
        at = pl.multiple_of(((g * 2 + half) * pieces + s) * piece, piece)
        out_buf[g, half, s] = result.astype(jnp.bfloat16)
        pltpu.make_async_copy(
            out_buf.at[g, half, s], out_hbm.at[:, pl.ds(at, piece)], out_sem.at[g, half, s]
        ).start()

    for half in range(2):
        for s in range(pieces):
            emit(f, half, s)
    if served <= steps:
        out_landed += serve(OUT, served)
        served += 1
    for half in range(2):
        own_wo[half].wait_recv()
        for s in range(pieces):
            emit(f_mate, half, s)

    for g, half, s in out_landed:
        emit(g, half, s)
    for t in range(steps + 2):
        if t >= served:
            for g, half, s in serve(OUT, t):
                emit(g, half, s)
        for g, half, s in gather_core(OUT, t):
            emit(g, half, s)

    for copy in started + own_wq + own_wo + [kv_mate]:
        copy.wait_send()
    for which, block in ((0, c), (1, c_mate)):
        for zz in range(1, pairs):
            @pl.when(zz > z)
            def _():
                kv_copy(which, block, zz).wait_send()
    for g in range(fsdp_size):
        for half in range(2):
            for s in range(pieces):
                at = ((g * 2 + half) * pieces + s) * piece
                pltpu.make_async_copy(
                    out_buf.at[g, half, s], out_hbm.at[:, pl.ds(at, piece)], out_sem.at[g, half, s]
                ).wait()


def per_device(ctx_size, fsdp_size, tokens, w_query, keys, values, gates, routes, w_out):
    rows, width = tokens.shape[1:]
    depth, inner = w_query.shape
    head_size = keys.shape[2]
    pieces = depth // (2 * piece)
    chips = fsdp_size // 2
    pairs = ctx_size // 2
    tables = [jnp.asarray(t) for t in rotary_tables(rows, ctx_size, head_size)]
    anywhere = pl.BlockSpec(memory_space=pl.ANY)
    bf16 = jnp.bfloat16
    dma = pltpu.SemaphoreType.DMA
    mixed = pl.pallas_call(
        functools.partial(kernel, ctx_size, fsdp_size, pieces),
        out_shape=jax.ShapeDtypeStruct((rows, width), bf16),
        in_specs=[anywhere] * 5 + [pl.BlockSpec(memory_space=pltpu.VMEM)] + [anywhere] * 3,
        out_specs=anywhere,
        scratch_shapes=[
            pltpu.VMEM((routes.shape[2], rows), jnp.int32),
            pltpu.VMEM(tables[0].shape, jnp.float32),
            pltpu.VMEM(tables[1].shape, jnp.float32),
            pltpu.VMEM((rows, width), bf16),
            pltpu.VMEM((fsdp_size, 2, pieces, piece, inner), bf16),
            pltpu.VMEM((fsdp_size, 2, pieces, inner, piece), bf16),
            pltpu.VMEM((ctx_size, rows, 2 * head_size), bf16),
            pltpu.VMEM((rows, inner), jnp.float32),
            pltpu.VMEM((rows, inner), bf16),
            pltpu.VMEM((rows, inner), bf16),
            pltpu.VMEM((fsdp_size, 2, pieces, rows, piece), bf16),
            dma((2, 8, chips - 1, pieces)),
            dma((2, 8, chips - 1, pieces)),
            dma((2, 2)),
            dma((2, 2)),
            dma((2, pairs)),
            dma((ctx_size,)),
            dma((4 + 2 * pieces,)),
            dma((2 * pieces,)),
            dma((fsdp_size, 2, pieces)),
            dma((3,)),
        ],
        compiler_params=pltpu.CompilerParams(
            collective_id=0, has_side_effects=True, vmem_limit_bytes=62 * 1024 * 1024
        ),
    )(
        tokens[0],
        w_query.reshape(2, pieces, piece, inner),
        keys[0],
        values[0],
        w_out,
        gates[0].T,
        routes[0].T,
        *tables,
    )
    return mixed[None]


def solution(mesh):
    in_specs = (
        P("fsdp", "ctx", None),
        P("fsdp", None),
        P("fsdp", "ctx", None),
        P("fsdp", "ctx", None),
        P("fsdp", "ctx", None),
        P("fsdp", "ctx", None),
        P(None, "fsdp"),
    )
    return jax.shard_map(
        functools.partial(per_device, mesh.shape["ctx"], mesh.shape["fsdp"]),
        mesh=mesh,
        in_specs=in_specs,
        out_specs=P("fsdp", "ctx", None),
        check_vma=False,
    )
```
